256 devices in a mesh: expert: 16 (over z, core), fsdp: 16 (over x, y).
Axes of the slice: x: 4, y: 4, z: 8, core: 2. Of those that a mesh axis runs over, the one named last changes fastest.
Arguments:
- grad_blocks: bfloat16 [16, 16, 512, 512], P('expert', None, 'fsdp'), may hold values from -42 to 42
- second_moment: float32 [16, 16, 512, 512], P('expert', None, 'fsdp'), may hold values from 0.1 to 2
- block_order: int32 [16, 16], P('expert'), may hold values from 0 to 15, as said below
- left_stat: float32 [256, 512, 512], P(('expert', 'fsdp')), may hold values from -1 to 3, as said below
- right_stat: float32 [256, 512, 512], P(('expert', 'fsdp')), may hold values from -1 to 3, as said below
- left_root: bfloat16 [256, 512, 512], P(('expert', 'fsdp')), may hold values from -1 to 2, as said below
- right_root: bfloat16 [256, 512, 512], P(('expert', 'fsdp')), may hold values from -1 to 2, as said below
Outputs:
- direction: float32 [16, 16, 512, 512], P('expert', None, 'fsdp')
- second_new: float32 [16, 16, 512, 512], P('expert', None, 'fsdp')
- left_stat_new: float32 [256, 512, 512], P(('expert', 'fsdp'))
- right_stat_new: float32 [256, 512, 512], P(('expert', 'fsdp'))
- left_root_new: bfloat16 [256, 512, 512], P(('expert', 'fsdp'))
- right_root_new: bfloat16 [256, 512, 512], P(('expert', 'fsdp'))
The draws below stay inside these ranges and needn't reach their ends.
Inputs may be any that keep to these rules, and one draw needn't show every extreme that they name: `block_order`: every row is a permutation of 0 to 15. `left_stat`: symmetric and positive definite. `right_stat`: symmetric and positive definite. `left_root`: symmetric. `right_root`: symmetric.
All inputs are finite; a program needn't handle non-finite values.
Results may differ from the reference program's by a relative error of at most 0.0049.
Values may be sent and summed in bfloat16 or wider, within the bound.
A program may use at most 64 MiB of HBM per device.

```python
import math
import jax
import jax.numpy as jnp
from jax import lax

BLK = 512
NBLK = 16
EXPERTS = 16
N_EXPERT = 16
N_FSDP = 16


def diag_values(key, salt):
    sub_key = jax.random.fold_in(key, salt)
    return jnp.exp(jax.random.uniform(sub_key, (EXPERTS * NBLK, BLK), minval=0.0, maxval=math.log(2.0)))


def symmetric_noise(key, scale):
    base = jnp.clip(jax.random.normal(key, (EXPERTS * NBLK, BLK, BLK)), -4.0, 4.0)
    return (base + jnp.swapaxes(base, 1, 2)) * (scale / math.sqrt(2.0 * BLK))


def draw_left_stat(key, part):
    diagonal = diag_values(key, 11)
    key = jax.random.fold_in(key, 21)
    return symmetric_noise(key, 0.4) + diagonal[:, :, None] * jnp.eye(BLK, dtype=jnp.float32)


def draw_right_stat(key, part):
    diagonal = diag_values(key, 12)
    key = jax.random.fold_in(key, 22)
    return symmetric_noise(key, 0.4) + diagonal[:, :, None] * jnp.eye(BLK, dtype=jnp.float32)


def draw_left_root(key, part):
    diagonal = diag_values(key, 11)
    key = jax.random.fold_in(key, 31)
    return (symmetric_noise(key, 0.1) + (diagonal ** (-0.25))[:, :, None] * jnp.eye(BLK, dtype=jnp.float32)).astype(jnp.bfloat16)


def draw_right_root(key, part):
    diagonal = diag_values(key, 12)
    key = jax.random.fold_in(key, 32)
    return (symmetric_noise(key, 0.1) + (diagonal ** (-0.25))[:, :, None] * jnp.eye(BLK, dtype=jnp.float32)).astype(jnp.bfloat16)


def draw_grad_blocks(key, part):
    key = jax.random.fold_in(key, 5)
    first, second, third = jax.random.split(key, 3)
    shape = (EXPERTS, NBLK, BLK, BLK)
    rise = 3.0 ** (jnp.arange(BLK, dtype=jnp.float32) / (BLK - 1)) / math.sqrt(3.0)
    row_scale = jnp.exp(jax.random.uniform(second, (EXPERTS, NBLK, BLK, 1), minval=math.log(0.3), maxval=math.log(3.0)))
    row_scale = row_scale * rise[None, None, :, None]
    col_scale = jnp.exp(jax.random.uniform(third, (EXPERTS, NBLK, 1, BLK), minval=math.log(0.5), maxval=math.log(2.0)))
    base = jnp.clip(jax.random.normal(first, shape), -4.0, 4.0)
    return (base * row_scale * col_scale).astype(jnp.bfloat16)


def draw_block_order(key, part):
    key = jax.random.fold_in(key, 7)
    keys = jax.random.split(key, EXPERTS)
    return jax.vmap(lambda sub_key: jax.random.permutation(sub_key, NBLK))(keys).astype(jnp.int32)


def steps_of(own_key, extent, cuts, smallest, top_value):
    factor_of, own = 1.0, jax.random.fold_in(own_key, 6)
    for dim, parts in cuts:
        draws = jnp.exp(jax.random.uniform(jax.random.fold_in(own, dim), (parts,), jnp.float32, smallest / len(cuts), top_value / len(cuts)))
        factor_of = factor_of * jnp.repeat(draws, extent[dim] // parts).reshape([-1 if axis == dim else 1 for axis in range(len(extent))])
    return factor_of


def setup_inputs(seed: int = 0) -> dict:
    arg_keys = jax.random.split(jax.random.key(seed), 8)
    grad_blocks = draw_grad_blocks(jax.random.fold_in(arg_keys[7], 71), 0)
    second_moment = jnp.clip(jnp.exp(math.log(2.0) - 2.9957323 * jax.random.uniform(arg_keys[1], (EXPERTS, NBLK, BLK, BLK), jnp.float32) ** steps_of(arg_keys[1], (EXPERTS, NBLK, BLK, BLK), ((0, 16), (2, 16)), -0.2, 0.2)), 0.1, 2.0)
    block_order = draw_block_order(jax.random.fold_in(arg_keys[7], 71), 0)
    left_stat = draw_left_stat(jax.random.fold_in(arg_keys[7], 71), 0)
    right_stat = draw_right_stat(jax.random.fold_in(arg_keys[7], 71), 0)
    left_root = draw_left_root(jax.random.fold_in(arg_keys[7], 71), 0)
    right_root = draw_right_root(jax.random.fold_in(arg_keys[7], 71), 0)
    return {"grad_blocks": grad_blocks, "second_moment": second_moment, "block_order": block_order, "left_stat": left_stat, "right_stat": right_stat, "left_root": left_root, "right_root": right_root}


def refine_root(root, stat):
    root_value = root.astype(jnp.float32)
    square = jnp.matmul(root, root, preferred_element_type=jnp.float32)
    fourth = jnp.matmul(square, square, precision=lax.Precision.HIGHEST)
    product = jnp.matmul(fourth, stat, precision=lax.Precision.HIGHEST)
    refined = 0.25 * (5.0 * root_value - jnp.matmul(root_value, product, precision=lax.Precision.HIGHEST))
    return refined.astype(jnp.bfloat16)

def one_block(pieces):
    gradient = pieces[0]
    gram_left = jnp.dot(gradient, gradient.T, preferred_element_type=jnp.float32)
    gram_right = jnp.dot(gradient.T, gradient, preferred_element_type=jnp.float32)
    left_new = 0.95 * pieces[1] + 0.05 / BLK * gram_left
    right_new = 0.95 * pieces[2] + 0.05 / BLK * gram_right
    half_step = jnp.dot(pieces[3], gradient, preferred_element_type=jnp.float32).astype(jnp.bfloat16)
    shaped = jnp.dot(half_step, pieces[4], preferred_element_type=jnp.float32).astype(jnp.bfloat16)
    return (left_new, right_new, refine_root(pieces[3], left_new), refine_root(pieces[4], right_new), shaped)

def reference(grad_blocks, second_moment, block_order, left_stat, right_stat, left_root, right_root):
    per_dev = NBLK // N_FSDP
    per_expert = NBLK // N_EXPERT
    slot_ids = jnp.arange(EXPERTS * NBLK, dtype=jnp.int32)
    device = slot_ids // per_dev
    within = slot_ids % per_dev
    column = device // N_FSDP
    row_index = device % N_FSDP
    item_index = row_index * per_dev + within
    expert = item_index // per_expert
    position = column * per_expert + item_index % per_expert
    chosen = block_order[expert, position].astype(jnp.int32)
    grad_values = grad_blocks.astype(jnp.float32)
    second_new = 0.95 * second_moment + 0.05 * grad_values * grad_values
    adam_step = grad_values / (jnp.sqrt(second_new) + 1e-08)
    adam_norm = lax.optimization_barrier(jnp.sum(adam_step * adam_step, axis=(2, 3)))
    owned_blocks = grad_blocks[expert, chosen]
    results = lax.map(one_block, (owned_blocks, left_stat, right_stat, left_root, right_root))
    shaped_home = jnp.zeros(grad_blocks.shape, jnp.bfloat16).at[expert, chosen].set(results[4])
    shaped_wide = shaped_home.astype(jnp.float32)
    shaped_norm = lax.optimization_barrier(jnp.sum(shaped_wide * shaped_wide, axis=(2, 3)))
    graft_ratio = jnp.sqrt(adam_norm / (shaped_norm + 1e-06))
    direction = graft_ratio[:, :, None, None] * shaped_wide
    return (direction, second_new, results[0], results[1], results[2], results[3])
```

```python
import functools

import jax
import jax.numpy as jnp
from jax import lax
from jax.experimental import pallas as pl
from jax.experimental.pallas import tpu as pltpu
from jax.sharding import PartitionSpec as P

MESH = pl.DeviceIdType.MESH
N = 16
ROWS = 32
BLK = 512
F32 = jnp.float32
BF16 = jnp.bfloat16


def dot(a, b, dims=((1,), (0,))):
    return lax.dot_general(a, b, (dims, ((), ())), preferred_element_type=F32)


def split(x):
    high = x.astype(BF16)
    return high, (x - high.astype(F32)).astype(BF16)


def near_peer(step, expert):
    m = step // 2
    dz = jnp.where(lax.rem(m, 2) == 1, (m + 1) // 2, 8 - m // 2)
    z = lax.rem(expert // 2 + dz, 8)
    return z * 2 + lax.rem(expert + step, 2)


def wait_bytes(ref, sem):
    pltpu.make_async_copy(ref, ref, sem).wait()


def exchange_kernel(
    order, grad_hbm, second_hbm, lstat_hbm, rstat_hbm, lroot_hbm, rroot_hbm,
    home, factor, second_new, stat_new, root_new,
    grad, second, stat, root, staged, block, shaped, passing, rows, part, parts, pow_hi, pow_lo,
    load_sem, scat_send, scat_recv, hop_send, hop_recv, home_send, home_recv, part_send, part_recv,
):
    e = lax.axis_index("expert")
    r = lax.axis_index("fsdp")
    diagonal = e == r

    loads = [
        pltpu.make_async_copy(grad_hbm, grad, load_sem.at[0]),
        pltpu.make_async_copy(second_hbm, second, load_sem.at[1]),
        pltpu.make_async_copy(lroot_hbm, root.at[0], load_sem.at[2]),
        pltpu.make_async_copy(rroot_hbm, root.at[1], load_sem.at[3]),
        pltpu.make_async_copy(lstat_hbm, stat.at[0], load_sem.at[4]),
        pltpu.make_async_copy(rstat_hbm, stat.at[1], load_sem.at[5]),
    ]
    for load in loads:
        load.start()

    barrier = pltpu.get_barrier_semaphore()

    @pl.loop(0, N)
    def _(i):
        @pl.when(jnp.logical_not(diagonal & (i == r)))
        def _():
            pl.semaphore_signal(barrier, inc=1, device_id=(r, i), device_id_type=MESH)

        @pl.when(i != r)
        def _():
            pl.semaphore_signal(barrier, inc=1, device_id=(e, i), device_id_type=MESH)

    loads[0].wait()

    @pl.loop(0, N)
    def _(i):
        staged[i] = grad[order[i]]

    pl.semaphore_wait(barrier, jnp.where(diagonal, 2 * N - 2, 2 * N - 1))

    @pl.loop(0, N)
    def _(k):
        i = near_peer(lax.rem(k + r, N), e)
        stays = diagonal & (i == e)

        @pl.when(jnp.logical_not(stays))
        def _():
            pltpu.make_async_remote_copy(
                staged.at[i], block.at[r], scat_send, scat_recv, device_id=(i, e), device_id_type=MESH
            ).start()

        @pl.when(stays)
        def _():
            pltpu.make_async_copy(staged.at[i], block.at[r], scat_recv).start()

    loads[1].wait()

    @pl.loop(0, N)
    def _(j):
        value = grad[j].astype(F32)
        moment = 0.95 * second[j] + 0.05 * value * value
        second_new[j] = moment
        step = value / (jnp.sqrt(moment) + 1e-08)
        rows[pl.ds(j, 1), :] = jnp.sum(step * step, axis=0, keepdims=True)

    diag_mask = lax.broadcasted_iota(jnp.int32, (N, 128), 0) == lax.broadcasted_iota(jnp.int32, (N, 128), 1)
    sums = jnp.sum(rows[...], axis=1, keepdims=True)
    part[...] = jnp.sum(jnp.where(diag_mask, sums, 0.0), axis=0, keepdims=True)
    parts[r] = part[...]

    @pl.loop(1, N)
    def _(k):
        pltpu.make_async_remote_copy(
            part, parts.at[r], part_send, part_recv, device_id=(e, lax.rem(r + k, N)), device_id_type=MESH
        ).start()

    loads[2].wait()
    loads[3].wait()

    @pl.loop(0, 2)
    def _(side):
        x = root[side]
        square_hi, square_lo = split(dot(x, x))
        cube_hi, cube_lo = split(dot(x, square_hi) + dot(x, square_lo))
        fifth = dot(cube_hi, square_hi) + dot(cube_hi, square_lo) + dot(cube_lo, square_hi)
        high, low = split(fifth)
        pow_hi[side] = high
        pow_lo[side] = low

    wait_bytes(block, scat_recv)
    g = block[...].reshape(BLK, BLK)
    half = dot(root[0], g).astype(BF16)
    step = dot(half, root[1])
    norm = jnp.sum(jnp.sum(step * step, axis=0, keepdims=True), axis=1, keepdims=True)
    scale = 1.0 / jnp.sqrt(norm + 1e-06)
    shaped[...] = (step * scale).astype(BF16).reshape(N, ROWS, BLK)

    @pl.loop(0, N)
    def _(k):
        i = lax.rem(r + k + e, N)

        @pl.when(i != r)
        def _():
            pltpu.make_async_remote_copy(
                shaped.at[i], passing.at[k], hop_send, hop_recv.at[k], device_id=(e, i), device_id_type=MESH
            ).start()

        @pl.when(i == r)
        def _():
            pltpu.make_async_copy(shaped.at[i], passing.at[k], hop_recv.at[k]).start()

    loads[4].wait()
    stat_new[0] = 0.95 * stat[0] + (0.05 / BLK) * dot(g, g, ((1,), (1,)))

    @pl.loop(0, N)
    def _(k):
        f = lax.rem(r + 2 * N - k - e, N)
        wait_bytes(passing.at[k], hop_recv.at[k])

        @pl.when(f != e)
        def _():
            pltpu.make_async_remote_copy(
                passing.at[k], home.at[e], home_send, home_recv, device_id=(f, r), device_id_type=MESH
            ).start()

        @pl.when(f == e)
        def _():
            pltpu.make_async_copy(passing.at[k], home.at[e], home_recv).start()

    loads[5].wait()
    stat_new[1] = 0.95 * stat[1] + (0.05 / BLK) * dot(g, g, ((0,), (0,)))

    @pl.loop(0, 2)
    def _(side):
        stat_hi, stat_lo = split(stat_new[side])
        product = dot(pow_hi[side], stat_hi) + dot(pow_hi[side], stat_lo) + dot(pow_lo[side], stat_hi)
        root_new[side] = (0.25 * (5.0 * root[side].astype(F32) - product)).astype(BF16)

    wait_bytes(parts.at[pl.ds(0, N - 1)], part_recv)
    total = jnp.sum(parts[...], axis=0)
    column = jnp.sum(jnp.where(diag_mask, total, 0.0), axis=1, keepdims=True)
    factor[...] = jnp.broadcast_to(jnp.sqrt(column), (N, BLK))

    wait_bytes(parts.at[pl.ds(0, N - 1)], part_send)

    @pl.when(diagonal)
    def _():
        wait_bytes(staged.at[pl.ds(0, N - 1)], scat_send)

    @pl.when(jnp.logical_not(diagonal))
    def _():
        wait_bytes(staged, scat_send)

    wait_bytes(shaped.at[pl.ds(0, N - 1)], hop_send)
    wait_bytes(passing.at[pl.ds(0, N - 1)], home_send)
    wait_bytes(home, home_recv)


def finish_kernel(
    order, home, factor, second_new, stat_new, root_new,
    direction, second_out, lstat_out, rstat_out, lroot_out, rroot_out,
    wide, sems,
):
    copies = [
        pltpu.make_async_copy(second_new, second_out, sems.at[0]),
        pltpu.make_async_copy(stat_new.at[0], lstat_out, sems.at[1]),
        pltpu.make_async_copy(stat_new.at[1], rstat_out, sems.at[2]),
        pltpu.make_async_copy(root_new.at[0], lroot_out, sems.at[3]),
        pltpu.make_async_copy(root_new.at[1], rroot_out, sems.at[4]),
    ]
    for copy in copies:
        copy.start()

    @pl.loop(0, N)
    def _(i):
        j = order[i]
        wide[j] = home[i].astype(F32) * factor[pl.ds(j, 1), :]

    last = pltpu.make_async_copy(wide, direction, sems.at[5])
    last.start()
    for copy in copies:
        copy.wait()
    last.wait()


def local(grad_blocks, second_moment, block_order, left_stat, right_stat, left_root, right_root):
    order = block_order[0]
    any_spec = pl.BlockSpec(memory_space=pl.ANY)
    vmem_spec = pl.BlockSpec(memory_space=pltpu.VMEM)
    smem_spec = pl.BlockSpec(memory_space=pltpu.SMEM)
    dma = pltpu.SemaphoreType.DMA
    piece = (N, ROWS, BLK)
    pair = (2, BLK, BLK)
    products = 2 * BLK**3
    results = pl.pallas_call(
        exchange_kernel,
        out_shape=[
            pltpu.VMEM(piece, BF16),
            pltpu.VMEM((N, BLK), F32),
            pltpu.VMEM(piece, F32),
            pltpu.VMEM(pair, F32),
            pltpu.VMEM(pair, BF16),
        ],
        in_specs=[smem_spec] + [any_spec] * 6,
        out_specs=[vmem_spec] * 5,
        scratch_shapes=[
            pltpu.VMEM(piece, BF16),
            pltpu.VMEM(piece, F32),
            pltpu.VMEM(pair, F32),
            pltpu.VMEM(pair, BF16),
            pltpu.VMEM(piece, BF16),
            pltpu.VMEM(piece, BF16),
            pltpu.VMEM(piece, BF16),
            pltpu.VMEM(piece, BF16),
            pltpu.VMEM((N, BLK), F32),
            pltpu.VMEM((1, 128), F32),
            pltpu.VMEM((N, 1, 128), F32),
            pltpu.VMEM(pair, BF16),
            pltpu.VMEM(pair, BF16),
            dma((6,)),
            dma,
            dma,
            dma,
            dma((N,)),
            dma,
            dma,
            dma,
            dma,
        ],
        compiler_params=pltpu.CompilerParams(
            collective_id=0, has_side_effects=True, vmem_limit_bytes=32 * 1024 * 1024
        ),
        cost_estimate=pl.CostEstimate(flops=22 * products, bytes_accessed=10 * 2**20, transcendentals=2**19),
        name="exchange",
    )(order, grad_blocks[0], second_moment[0], left_stat[0], right_stat[0], left_root[0], right_root[0])
    outs = pl.pallas_call(
        finish_kernel,
        out_shape=[
            jax.ShapeDtypeStruct(piece, F32),
            jax.ShapeDtypeStruct(piece, F32),
            jax.ShapeDtypeStruct((BLK, BLK), F32),
            jax.ShapeDtypeStruct((BLK, BLK), F32),
            jax.ShapeDtypeStruct((BLK, BLK), BF16),
            jax.ShapeDtypeStruct((BLK, BLK), BF16),
        ],
        in_specs=[smem_spec] + [vmem_spec] * 5,
        out_specs=[any_spec] * 6,
        scratch_shapes=[pltpu.VMEM(piece, F32), dma((6,))],
        compiler_params=pltpu.CompilerParams(vmem_limit_bytes=32 * 1024 * 1024),
        cost_estimate=pl.CostEstimate(flops=2**19, bytes_accessed=10 * 2**20, transcendentals=0),
        name="finish",
    )(order, *results)
    return tuple(out[None] for out in outs)


def solution(mesh):
    placed = (
        P("expert", None, "fsdp", None),
        P("expert", None, "fsdp", None),
        P("expert", None),
        P(("expert", "fsdp"), None, None),
        P(("expert", "fsdp"), None, None),
        P(("expert", "fsdp"), None, None),
        P(("expert", "fsdp"), None, None),
    )
    return jax.shard_map(
        local,
        mesh=mesh,
        in_specs=placed,
        out_specs=(
            P("expert", None, "fsdp", None),
            P("expert", None, "fsdp", None),
            P(("expert", "fsdp"), None, None),
            P(("expert", "fsdp"), None, None),
            P(("expert", "fsdp"), None, None),
            P(("expert", "fsdp"), None, None),
        ),
        check_vma=False,
    )
```

```python
import functools

import jax
import jax.numpy as jnp
from jax import lax
from jax.experimental import pallas as pl
from jax.experimental.pallas import tpu as pltpu
from jax.sharding import PartitionSpec as P

MESH = pl.DeviceIdType.MESH
N = 16
ROWS = 32
BLK = 512
F32 = jnp.float32
BF16 = jnp.bfloat16


def dot(a, b, dims=((1,), (0,))):
    return lax.dot_general(a, b, (dims, ((), ())), preferred_element_type=F32)


def split(x):
    high = x.astype(BF16)
    return high, (x - high.astype(F32)).astype(BF16)


def target(step, expert, turn):
    m = lax.rem(lax.rem(step, 8) + turn, 8)
    dz = jnp.where(lax.rem(m, 2) == 1, (m + 1) // 2, 8 - m // 2)
    return lax.rem(expert // 2 + dz, 8) * 2 + step // 8


def wait_bytes(ref, sem):
    pltpu.make_async_copy(ref, ref, sem).wait()


def exchange_kernel(
    order_hbm, grad_hbm, second_hbm, lstat_hbm, rstat_hbm, lroot_hbm, rroot_hbm,
    home, factor, second_new, stat_new, root_new,
    order, grad, second, stat, root, staged, block, shaped, passing, rows, part, parts, pow_hi, pow_lo,
    load_sem, scat_send, scat_recv, hop_send, hop_recv, home_send, home_recv, part_send, part_recv, here_sem, go_sem,
):
    e = lax.axis_index("expert")
    r = lax.axis_index("fsdp")
    diagonal = e == r

    barrier = pltpu.get_barrier_semaphore()

    @pl.loop(0, N)
    def _(i):
        @pl.when(jnp.logical_not(diagonal & (i == r)))
        def _():
            pl.semaphore_signal(barrier, inc=1, device_id=(r, i), device_id_type=MESH)

    loads = [
        pltpu.make_async_copy(grad_hbm, grad, load_sem.at[0]),
        pltpu.make_async_copy(second_hbm, second, load_sem.at[1]),
        pltpu.make_async_copy(lroot_hbm, root.at[0], load_sem.at[2]),
        pltpu.make_async_copy(rroot_hbm, root.at[1], load_sem.at[3]),
        pltpu.make_async_copy(lstat_hbm, stat.at[0], load_sem.at[4]),
        pltpu.make_async_copy(rstat_hbm, stat.at[1], load_sem.at[5]),
    ]
    load_order = pltpu.make_async_copy(order_hbm, order, load_sem.at[6])
    load_order.start()
    for load in loads:
        load.start()

    load_order.wait()
    loads[0].wait()

    @pl.loop(0, N)
    def _(i):
        staged[i] = grad[order[0, i]]

    pl.semaphore_wait(barrier, jnp.where(diagonal, N - 1, N))

    @pl.loop(0, N)
    def _(k):
        i = target(k, e, r)
        stays = diagonal & (i == e)

        @pl.when(jnp.logical_not(stays))
        def _():
            pltpu.make_async_remote_copy(
                staged.at[i], block.at[r], scat_send, scat_recv, device_id=(i, e), device_id_type=MESH
            ).start()

        @pl.when(stays)
        def _():
            pltpu.make_async_copy(staged.at[i], block.at[r], scat_recv).start()

    @pl.when(jnp.logical_not(diagonal))
    def _():
        pl.semaphore_signal(here_sem, inc=1, device_id=(e, e), device_id_type=MESH)

    loads[1].wait()

    @pl.loop(0, N)
    def _(j):
        value = grad[j].astype(F32)
        moment = 0.95 * second[j] + 0.05 * value * value
        second_new[j] = moment
        step = value / (jnp.sqrt(moment) + 1e-08)
        rows[pl.ds(j, 1), :] = jnp.sum(step * step, axis=0, keepdims=True)

    diag_mask = lax.broadcasted_iota(jnp.int32, (N, 128), 0) == lax.broadcasted_iota(jnp.int32, (N, 128), 1)
    sums = jnp.sum(rows[...], axis=1, keepdims=True)
    part[...] = jnp.sum(jnp.where(diag_mask, sums, 0.0), axis=0, keepdims=True)
    parts[r] = part[...]

    @pl.when(diagonal)
    def _():
        pl.semaphore_wait(here_sem, N - 1)

        @pl.loop(1, N)
        def _(k):
            pl.semaphore_signal(go_sem, inc=1, device_id=(e, lax.rem(r + k, N)), device_id_type=MESH)

    loads[2].wait()
    loads[3].wait()

    @pl.loop(0, 2)
    def _(side):
        x = root[side]
        square_hi, square_lo = split(dot(x, x))
        cube_hi, cube_lo = split(dot(x, square_hi) + dot(x, square_lo))
        fifth = dot(cube_hi, square_hi) + dot(cube_hi, square_lo) + dot(cube_lo, square_hi)
        high, low = split(fifth)
        pow_hi[side] = high
        pow_lo[side] = low

    @pl.when(jnp.logical_not(diagonal))
    def _():
        pl.semaphore_wait(go_sem, 1)

    @pl.loop(1, N)
    def _(k):
        pltpu.make_async_remote_copy(
            part, parts.at[r], part_send, part_recv, device_id=(e, lax.rem(r + k, N)), device_id_type=MESH
        ).start()

    wait_bytes(block, scat_recv)
    g = block[...].reshape(BLK, BLK)
    half = dot(root[0], g).astype(BF16)
    step = dot(half, root[1])
    norm = jnp.sum(jnp.sum(step * step, axis=0, keepdims=True), axis=1, keepdims=True)
    scale = 1.0 / jnp.sqrt(norm + 1e-06)
    shaped[...] = (step * scale).astype(BF16).reshape(N, ROWS, BLK)

    @pl.loop(0, N)
    def _(k):
        i = lax.rem(r + k + e, N)

        @pl.when(i != r)
        def _():
            pltpu.make_async_remote_copy(
                shaped.at[i], passing.at[k], hop_send, hop_recv.at[k], device_id=(e, i), device_id_type=MESH
            ).start()

        @pl.when(i == r)
        def _():
            pltpu.make_async_copy(shaped.at[i], passing.at[k], hop_recv.at[k]).start()

    loads[4].wait()
    stat_new[0] = 0.95 * stat[0] + (0.05 / BLK) * dot(g, g, ((1,), (1,)))

    @pl.loop(0, N)
    def _(k):
        f = lax.rem(r + 2 * N - k - e, N)
        wait_bytes(passing.at[k], hop_recv.at[k])

        @pl.when(f != e)
        def _():
            pltpu.make_async_remote_copy(
                passing.at[k], home.at[e], home_send, home_recv, device_id=(f, r), device_id_type=MESH
            ).start()

        @pl.when(f == e)
        def _():
            pltpu.make_async_copy(passing.at[k], home.at[e], home_recv).start()

    loads[5].wait()
    stat_new[1] = 0.95 * stat[1] + (0.05 / BLK) * dot(g, g, ((0,), (0,)))

    @pl.loop(0, 2)
    def _(side):
        stat_hi, stat_lo = split(stat_new[side])
        product = dot(pow_hi[side], stat_hi) + dot(pow_hi[side], stat_lo) + dot(pow_lo[side], stat_hi)
        root_new[side] = (0.25 * (5.0 * root[side].astype(F32) - product)).astype(BF16)

    wait_bytes(parts.at[pl.ds(0, N - 1)], part_recv)
    total = jnp.sum(parts[...], axis=0)
    column = jnp.sum(jnp.where(diag_mask, total, 0.0), axis=1, keepdims=True)
    factor[...] = jnp.broadcast_to(jnp.sqrt(column), (N, BLK))

    wait_bytes(parts.at[pl.ds(0, N - 1)], part_send)

    @pl.when(diagonal)
    def _():
        wait_bytes(staged.at[pl.ds(0, N - 1)], scat_send)

    @pl.when(jnp.logical_not(diagonal))
    def _():
        wait_bytes(staged, scat_send)

    wait_bytes(shaped.at[pl.ds(0, N - 1)], hop_send)
    wait_bytes(passing.at[pl.ds(0, N - 1)], home_send)
    wait_bytes(home, home_recv)


def finish_kernel(
    order, home, factor, second_new, stat_new, root_new,
    direction, second_out, lstat_out, rstat_out, lroot_out, rroot_out,
    wide, sems,
):
    copies = [
        pltpu.make_async_copy(second_new, second_out, sems.at[0]),
        pltpu.make_async_copy(stat_new.at[0], lstat_out, sems.at[1]),
        pltpu.make_async_copy(stat_new.at[1], rstat_out, sems.at[2]),
        pltpu.make_async_copy(root_new.at[0], lroot_out, sems.at[3]),
        pltpu.make_async_copy(root_new.at[1], rroot_out, sems.at[4]),
    ]
    for copy in copies:
        copy.start()

    @pl.loop(0, N)
    def _(i):
        j = order[i]
        wide[j] = home[i].astype(F32) * factor[pl.ds(j, 1), :]

    last = pltpu.make_async_copy(wide, direction, sems.at[5])
    last.start()
    for copy in copies:
        copy.wait()
    last.wait()


def local(grad_blocks, second_moment, block_order, left_stat, right_stat, left_root, right_root):
    order = block_order[0]
    any_spec = pl.BlockSpec(memory_space=pl.ANY)
    hbm_spec = pl.BlockSpec(memory_space=pltpu.HBM)
    vmem_spec = pl.BlockSpec(memory_space=pltpu.VMEM)
    smem_spec = pl.BlockSpec(memory_space=pltpu.SMEM)
    dma = pltpu.SemaphoreType.DMA
    piece = (N, ROWS, BLK)
    pair = (2, BLK, BLK)
    products = 2 * BLK**3
    results = pl.pallas_call(
        exchange_kernel,
        out_shape=[
            pltpu.VMEM(piece, BF16),
            pltpu.VMEM((N, BLK), F32),
            pltpu.VMEM(piece, F32),
            pltpu.VMEM(pair, F32),
            pltpu.VMEM(pair, BF16),
        ],
        in_specs=[hbm_spec] * 7,
        out_specs=[vmem_spec] * 5,
        scratch_shapes=[
            pltpu.SMEM((1, N), jnp.int32),
            pltpu.VMEM(piece, BF16),
            pltpu.VMEM(piece, F32),
            pltpu.VMEM(pair, F32),
            pltpu.VMEM(pair, BF16),
            pltpu.VMEM(piece, BF16),
            pltpu.VMEM(piece, BF16),
            pltpu.VMEM(piece, BF16),
            pltpu.VMEM(piece, BF16),
            pltpu.VMEM((N, BLK), F32),
            pltpu.VMEM((1, 128), F32),
            pltpu.VMEM((N, 1, 128), F32),
            pltpu.VMEM(pair, BF16),
            pltpu.VMEM(pair, BF16),
            dma((7,)),
            dma,
            dma,
            dma,
            dma((N,)),
            dma,
            dma,
            dma,
            dma,
            pltpu.SemaphoreType.REGULAR,
            pltpu.SemaphoreType.REGULAR,
        ],
        compiler_params=pltpu.CompilerParams(
            collective_id=0, has_side_effects=True, vmem_limit_bytes=32 * 1024 * 1024
        ),
        cost_estimate=pl.CostEstimate(flops=22 * products, bytes_accessed=10 * 2**20, transcendentals=2**19),
        name="exchange",
    )(
        pltpu.with_memory_space_constraint(block_order, pltpu.HBM),
        *(
            pltpu.with_memory_space_constraint(x[0], pltpu.HBM)
            for x in (grad_blocks, second_moment, left_stat, right_stat, left_root, right_root)
        ),
    )
    outs = pl.pallas_call(
        finish_kernel,
        out_shape=[
            jax.ShapeDtypeStruct(piece, F32),
            jax.ShapeDtypeStruct(piece, F32),
            jax.ShapeDtypeStruct((BLK, BLK), F32),
            jax.ShapeDtypeStruct((BLK, BLK), F32),
            jax.ShapeDtypeStruct((BLK, BLK), BF16),
            jax.ShapeDtypeStruct((BLK, BLK), BF16),
        ],
        in_specs=[smem_spec] + [vmem_spec] * 5,
        out_specs=[any_spec] * 6,
        scratch_shapes=[pltpu.VMEM(piece, F32), dma((6,))],
        compiler_params=pltpu.CompilerParams(vmem_limit_bytes=32 * 1024 * 1024),
        cost_estimate=pl.CostEstimate(flops=2**19, bytes_accessed=10 * 2**20, transcendentals=0),
        name="finish",
    )(order, *results)
    return tuple(out[None] for out in outs)


def solution(mesh):
    placed = (
        P("expert", None, "fsdp", None),
        P("expert", None, "fsdp", None),
        P("expert", None),
        P(("expert", "fsdp"), None, None),
        P(("expert", "fsdp"), None, None),
        P(("expert", "fsdp"), None, None),
        P(("expert", "fsdp"), None, None),
    )
    return jax.shard_map(
        local,
        mesh=mesh,
        in_specs=placed,
        out_specs=(
            P("expert", None, "fsdp", None),
            P("expert", None, "fsdp", None),
            P(("expert", "fsdp"), None, None),
            P(("expert", "fsdp"), None, None),
            P(("expert", "fsdp"), None, None),
            P(("expert", "fsdp"), None, None),
        ),
        check_vma=False,
    )
```

```python
import functools

import jax
import jax.numpy as jnp
from jax import lax
from jax.experimental import pallas as pl
from jax.experimental.pallas import tpu as pltpu
from jax.sharding import PartitionSpec as P

MESH = pl.DeviceIdType.MESH
N = 16
ROWS = 32
BLK = 512
F32 = jnp.float32
BF16 = jnp.bfloat16


def dot(a, b, dims=((1,), (0,))):
    return lax.dot_general(a, b, (dims, ((), ())), preferred_element_type=F32)


def split(x):
    high = x.astype(BF16)
    return high, (x - high.astype(F32)).astype(BF16)


def pick(index, values):
    result = values[-1]
    for at, value in enumerate(values[:-1]):
        result = jnp.where(index == at, value, result)
    return result


def target(step, expert, turn):
    m = lax.rem(step, 4) + turn
    far = pick(lax.rem(m, 4), (4, 3, 5, 6))
    near = pick(lax.rem(m, 4), (2, 1, 7, 0))
    dz = jnp.where(lax.rem(step, 8) < 4, far, near)
    return lax.rem(expert // 2 + dz, 8) * 2 + step // 8


def wait_bytes(ref, sem):
    pltpu.make_async_copy(ref, ref, sem).wait()


def exchange_kernel(
    order_hbm, grad_hbm, second_hbm, lstat_hbm, rstat_hbm, lroot_hbm, rroot_hbm,
    home, factor, second_new, stat_new, root_new,
    order, grad, second, stat, root, staged, block, shaped, passing, rows, part, parts, pow_hi, pow_lo,
    load_sem, scat_send, scat_recv, hop_send, hop_recv, home_send, home_recv, part_send, part_recv, here_sem, go_sem,
):
    e = lax.axis_index("expert")
    r = lax.axis_index("fsdp")
    diagonal = e == r

    barrier = pltpu.get_barrier_semaphore()

    @pl.loop(0, N)
    def _(i):
        @pl.when(jnp.logical_not(diagonal & (i == r)))
        def _():
            pl.semaphore_signal(barrier, inc=1, device_id=(r, i), device_id_type=MESH)

    loads = [
        pltpu.make_async_copy(grad_hbm, grad, load_sem.at[0]),
        pltpu.make_async_copy(second_hbm, second, load_sem.at[1]),
        pltpu.make_async_copy(lroot_hbm, root.at[0], load_sem.at[2]),
        pltpu.make_async_copy(rroot_hbm, root.at[1], load_sem.at[3]),
        pltpu.make_async_copy(lstat_hbm, stat.at[0], load_sem.at[4]),
        pltpu.make_async_copy(rstat_hbm, stat.at[1], load_sem.at[5]),
    ]
    load_order = pltpu.make_async_copy(order_hbm, order, load_sem.at[6])
    load_order.start()
    for load in loads:
        load.start()

    load_order.wait()
    loads[0].wait()

    @pl.loop(0, N)
    def _(i):
        staged[i] = grad[order[0, i]]

    pl.semaphore_wait(barrier, jnp.where(diagonal, N - 1, N))

    @pl.loop(0, N)
    def _(k):
        i = target(k, e, r)
        stays = diagonal & (i == e)

        @pl.when(jnp.logical_not(stays))
        def _():
            pltpu.make_async_remote_copy(
                staged.at[i], block.at[r], scat_send, scat_recv, device_id=(i, e), device_id_type=MESH
            ).start()

        @pl.when(stays)
        def _():
            pltpu.make_async_copy(staged.at[i], block.at[r], scat_recv).start()

    @pl.when(jnp.logical_not(diagonal))
    def _():
        pl.semaphore_signal(here_sem, inc=1, device_id=(e, e), device_id_type=MESH)

    loads[1].wait()

    @pl.loop(0, N)
    def _(j):
        value = grad[j].astype(F32)
        moment = 0.95 * second[j] + 0.05 * value * value
        second_new[j] = moment
        step = value / (jnp.sqrt(moment) + 1e-08)
        rows[pl.ds(j, 1), :] = jnp.sum(step * step, axis=0, keepdims=True)

    diag_mask = lax.broadcasted_iota(jnp.int32, (N, 128), 0) == lax.broadcasted_iota(jnp.int32, (N, 128), 1)
    sums = jnp.sum(rows[...], axis=1, keepdims=True)
    part[...] = jnp.sum(jnp.where(diag_mask, sums, 0.0), axis=0, keepdims=True)
    parts[r] = part[...]

    @pl.when(diagonal)
    def _():
        pl.semaphore_wait(here_sem, N - 1)

        @pl.loop(1, N)
        def _(k):
            pl.semaphore_signal(go_sem, inc=1, device_id=(e, lax.rem(r + k, N)), device_id_type=MESH)

    loads[2].wait()
    loads[3].wait()

    @pl.loop(0, 2)
    def _(side):
        x = root[side]
        square_hi, square_lo = split(dot(x, x))
        cube_hi, cube_lo = split(dot(x, square_hi) + dot(x, square_lo))
        fifth = dot(cube_hi, square_hi) + dot(cube_hi, square_lo) + dot(cube_lo, square_hi)
        high, low = split(fifth)
        pow_hi[side] = high
        pow_lo[side] = low

    @pl.when(jnp.logical_not(diagonal))
    def _():
        pl.semaphore_wait(go_sem, 1)

    @pl.loop(1, N)
    def _(k):
        pltpu.make_async_remote_copy(
            part, parts.at[r], part_send, part_recv, device_id=(e, lax.rem(r + k, N)), device_id_type=MESH
        ).start()

    wait_bytes(block, scat_recv)
    g = block[...].reshape(BLK, BLK)
    half = dot(root[0], g).astype(BF16)
    step = dot(half, root[1])
    norm = jnp.sum(jnp.sum(step * step, axis=0, keepdims=True), axis=1, keepdims=True)
    scale = 1.0 / jnp.sqrt(norm + 1e-06)
    shaped[...] = (step * scale).astype(BF16).reshape(N, ROWS, BLK)

    @pl.loop(0, N)
    def _(k):
        i = lax.rem(r + k + e, N)

        @pl.when(i != r)
        def _():
            pltpu.make_async_remote_copy(
                shaped.at[i], passing.at[k], hop_send, hop_recv.at[k], device_id=(e, i), device_id_type=MESH
            ).start()

        @pl.when(i == r)
        def _():
            pltpu.make_async_copy(shaped.at[i], passing.at[k], hop_recv.at[k]).start()

    loads[4].wait()
    stat_new[0] = 0.95 * stat[0] + (0.05 / BLK) * dot(g, g, ((1,), (1,)))

    @pl.loop(0, N)
    def _(k):
        f = lax.rem(r + 2 * N - k - e, N)
        wait_bytes(passing.at[k], hop_recv.at[k])

        @pl.when(f != e)
        def _():
            pltpu.make_async_remote_copy(
                passing.at[k], home.at[e], home_send, home_recv, device_id=(f, r), device_id_type=MESH
            ).start()

        @pl.when(f == e)
        def _():
            pltpu.make_async_copy(passing.at[k], home.at[e], home_recv).start()

    loads[5].wait()
    stat_new[1] = 0.95 * stat[1] + (0.05 / BLK) * dot(g, g, ((0,), (0,)))

    @pl.loop(0, 2)
    def _(side):
        stat_hi, stat_lo = split(stat_new[side])
        product = dot(pow_hi[side], stat_hi) + dot(pow_hi[side], stat_lo) + dot(pow_lo[side], stat_hi)
        root_new[side] = (0.25 * (5.0 * root[side].astype(F32) - product)).astype(BF16)

    wait_bytes(parts.at[pl.ds(0, N - 1)], part_recv)
    total = jnp.sum(parts[...], axis=0)
    column = jnp.sum(jnp.where(diag_mask, total, 0.0), axis=1, keepdims=True)
    factor[...] = jnp.broadcast_to(jnp.sqrt(column), (N, BLK))

    wait_bytes(parts.at[pl.ds(0, N - 1)], part_send)

    @pl.when(diagonal)
    def _():
        wait_bytes(staged.at[pl.ds(0, N - 1)], scat_send)

    @pl.when(jnp.logical_not(diagonal))
    def _():
        wait_bytes(staged, scat_send)

    wait_bytes(shaped.at[pl.ds(0, N - 1)], hop_send)
    wait_bytes(passing.at[pl.ds(0, N - 1)], home_send)
    wait_bytes(home, home_recv)


def finish_kernel(
    order_hbm, home, factor, second_new, stat_new, root_new,
    direction, second_out, lstat_out, rstat_out, lroot_out, rroot_out,
    order, wide, sems,
):
    load = pltpu.make_async_copy(order_hbm, order, sems.at[6])
    load.start()
    copies = [
        pltpu.make_async_copy(second_new, second_out, sems.at[0]),
        pltpu.make_async_copy(stat_new.at[0], lstat_out, sems.at[1]),
        pltpu.make_async_copy(stat_new.at[1], rstat_out, sems.at[2]),
        pltpu.make_async_copy(root_new.at[0], lroot_out, sems.at[3]),
        pltpu.make_async_copy(root_new.at[1], rroot_out, sems.at[4]),
    ]
    for copy in copies:
        copy.start()

    load.wait()

    @pl.loop(0, N)
    def _(i):
        j = order[0, i]
        wide[j] = home[i].astype(F32) * factor[pl.ds(j, 1), :]

    last = pltpu.make_async_copy(wide, direction, sems.at[5])
    last.start()
    for copy in copies:
        copy.wait()
    last.wait()


def local(grad_blocks, second_moment, block_order, left_stat, right_stat, left_root, right_root):
    order = pltpu.with_memory_space_constraint(block_order, pltpu.HBM)
    any_spec = pl.BlockSpec(memory_space=pl.ANY)
    hbm_spec = pl.BlockSpec(memory_space=pltpu.HBM)
    vmem_spec = pl.BlockSpec(memory_space=pltpu.VMEM)
    dma = pltpu.SemaphoreType.DMA
    piece = (N, ROWS, BLK)
    pair = (2, BLK, BLK)
    products = 2 * BLK**3
    results = pl.pallas_call(
        exchange_kernel,
        out_shape=[
            pltpu.VMEM(piece, BF16),
            pltpu.VMEM((N, BLK), F32),
            pltpu.VMEM(piece, F32),
            pltpu.VMEM(pair, F32),
            pltpu.VMEM(pair, BF16),
        ],
        in_specs=[hbm_spec] * 7,
        out_specs=[vmem_spec] * 5,
        scratch_shapes=[
            pltpu.SMEM((1, N), jnp.int32),
            pltpu.VMEM(piece, BF16),
            pltpu.VMEM(piece, F32),
            pltpu.VMEM(pair, F32),
            pltpu.VMEM(pair, BF16),
            pltpu.VMEM(piece, BF16),
            pltpu.VMEM(piece, BF16),
            pltpu.VMEM(piece, BF16),
            pltpu.VMEM(piece, BF16),
            pltpu.VMEM((N, BLK), F32),
            pltpu.VMEM((1, 128), F32),
            pltpu.VMEM((N, 1, 128), F32),
            pltpu.VMEM(pair, BF16),
            pltpu.VMEM(pair, BF16),
            dma((7,)),
            dma,
            dma,
            dma,
            dma((N,)),
            dma,
            dma,
            dma,
            dma,
            pltpu.SemaphoreType.REGULAR,
            pltpu.SemaphoreType.REGULAR,
        ],
        compiler_params=pltpu.CompilerParams(
            collective_id=0, has_side_effects=True, vmem_limit_bytes=32 * 1024 * 1024
        ),
        cost_estimate=pl.CostEstimate(flops=22 * products, bytes_accessed=10 * 2**20, transcendentals=2**19),
        name="exchange",
    )(
        order,
        *(
            pltpu.with_memory_space_constraint(x[0], pltpu.HBM)
            for x in (grad_blocks, second_moment, left_stat, right_stat, left_root, right_root)
        ),
    )
    outs = pl.pallas_call(
        finish_kernel,
        out_shape=[
            jax.ShapeDtypeStruct(piece, F32),
            jax.ShapeDtypeStruct(piece, F32),
            jax.ShapeDtypeStruct((BLK, BLK), F32),
            jax.ShapeDtypeStruct((BLK, BLK), F32),
            jax.ShapeDtypeStruct((BLK, BLK), BF16),
            jax.ShapeDtypeStruct((BLK, BLK), BF16),
        ],
        in_specs=[hbm_spec] + [vmem_spec] * 5,
        out_specs=[any_spec] * 6,
        scratch_shapes=[pltpu.SMEM((1, N), jnp.int32), pltpu.VMEM(piece, F32), dma((7,))],
        compiler_params=pltpu.CompilerParams(vmem_limit_bytes=32 * 1024 * 1024),
        cost_estimate=pl.CostEstimate(flops=2**19, bytes_accessed=10 * 2**20, transcendentals=0),
        name="finish",
    )(order, *results)
    return tuple(out[None] for out in outs)


def solution(mesh):
    placed = (
        P("expert", None, "fsdp", None),
        P("expert", None, "fsdp", None),
        P("expert", None),
        P(("expert", "fsdp"), None, None),
        P(("expert", "fsdp"), None, None),
        P(("expert", "fsdp"), None, None),
        P(("expert", "fsdp"), None, None),
    )
    return jax.shard_map(
        local,
        mesh=mesh,
        in_specs=placed,
        out_specs=(
            P("expert", None, "fsdp", None),
            P("expert", None, "fsdp", None),
            P(("expert", "fsdp"), None, None),
            P(("expert", "fsdp"), None, None),
            P(("expert", "fsdp"), None, None),
            P(("expert", "fsdp"), None, None),
        ),
        check_vma=False,
    )
```

```python
import functools

import jax
import jax.numpy as jnp
from jax import lax
from jax.experimental import pallas as pl
from jax.experimental.pallas import tpu as pltpu
from jax.sharding import PartitionSpec as P

MESH = pl.DeviceIdType.MESH
N = 16
ROWS = 32
BLK = 512
F32 = jnp.float32
BF16 = jnp.bfloat16


def dot(a, b, dims=((1,), (0,))):
    return lax.dot_general(a, b, (dims, ((), ())), preferred_element_type=F32)


def split(x):
    high = x.astype(BF16)
    return high, (x - high.astype(F32)).astype(BF16)


def pick(index, values):
    result = values[-1]
    for at, value in enumerate(values[:-1]):
        result = jnp.where(index == at, value, result)
    return result


def target(step, expert, turn):
    m = lax.rem(step, 4) + turn
    far = pick(lax.rem(m, 4), (4, 3, 5, 6))
    near = pick(lax.rem(m, 4), (2, 1, 7, 0))
    dz = jnp.where(lax.rem(step, 8) < 4, far, near)
    return lax.rem(expert // 2 + dz, 8) * 2 + step // 8


def wait_bytes(ref, sem):
    pltpu.make_async_copy(ref, ref, sem).wait()


def exchange_kernel(
    order_hbm, grad_hbm, second_hbm, lstat_hbm, rstat_hbm, lroot_hbm, rroot_hbm,
    home, factor, second_new, stat_new, root_new,
    order, grad, second, stat, root, staged, block, half, wide, shaped, passing, rows, part, parts, pow_hi, pow_lo,
    load_sem, scat_send, scat_recv, hop_send, hop_recv, home_send, home_recv, part_send, part_recv, here_sem, go_sem,
):
    e = lax.axis_index("expert")
    r = lax.axis_index("fsdp")
    diagonal = e == r

    loads = [
        pltpu.make_async_copy(grad_hbm, grad, load_sem.at[0]),
        pltpu.make_async_copy(second_hbm, second, load_sem.at[1]),
        pltpu.make_async_copy(lroot_hbm, root.at[0], load_sem.at[2]),
        pltpu.make_async_copy(rroot_hbm, root.at[1], load_sem.at[3]),
        pltpu.make_async_copy(lstat_hbm, stat.at[0], load_sem.at[4]),
        pltpu.make_async_copy(rstat_hbm, stat.at[1], load_sem.at[5]),
    ]
    load_order = pltpu.make_async_copy(order_hbm, order, load_sem.at[6])
    load_order.start()
    loads[0].start()

    barrier = pltpu.get_barrier_semaphore()

    @pl.loop(0, N)
    def _(i):
        @pl.when(jnp.logical_not(diagonal & (i == r)))
        def _():
            pl.semaphore_signal(barrier, inc=1, device_id=(r, i), device_id_type=MESH)

    for load in loads[1:]:
        load.start()

    load_order.wait()
    loads[0].wait()

    @pl.loop(0, N)
    def _(i):
        staged[i] = grad[order[0, i]]

    pl.semaphore_wait(barrier, jnp.where(diagonal, N - 1, N))

    @pl.loop(0, N)
    def _(k):
        i = target(k, e, r)
        stays = diagonal & (i == e)

        @pl.when(jnp.logical_not(stays))
        def _():
            pltpu.make_async_remote_copy(
                staged.at[i], block.at[r], scat_send, scat_recv, device_id=(i, e), device_id_type=MESH
            ).start()

        @pl.when(stays)
        def _():
            pltpu.make_async_copy(staged.at[i], block.at[r], scat_recv).start()

    @pl.when(jnp.logical_not(diagonal))
    def _():
        pl.semaphore_signal(here_sem, inc=1, device_id=(e, e), device_id_type=MESH)

    loads[1].wait()

    @pl.loop(0, N)
    def _(j):
        value = grad[j].astype(F32)
        moment = 0.95 * second[j] + 0.05 * value * value
        second_new[j] = moment
        step = value / (jnp.sqrt(moment) + 1e-08)
        rows[pl.ds(j, 1), :] = jnp.sum(step * step, axis=0, keepdims=True)

    diag_mask = lax.broadcasted_iota(jnp.int32, (N, 128), 0) == lax.broadcasted_iota(jnp.int32, (N, 128), 1)
    sums = jnp.sum(rows[...], axis=1, keepdims=True)
    part[...] = jnp.sum(jnp.where(diag_mask, sums, 0.0), axis=0, keepdims=True)
    parts[r] = part[...]

    @pl.when(diagonal)
    def _():
        pl.semaphore_wait(here_sem, N - 1)

        @pl.loop(1, N)
        def _(k):
            pl.semaphore_signal(go_sem, inc=1, device_id=(e, lax.rem(r + k, N)), device_id_type=MESH)

    loads[2].wait()
    loads[3].wait()

    @pl.loop(0, 2)
    def _(side):
        x = root[side]
        square_hi, square_lo = split(dot(x, x))
        cube_hi, cube_lo = split(dot(x, square_hi) + dot(x, square_lo))
        fifth = dot(cube_hi, square_hi) + dot(cube_hi, square_lo) + dot(cube_lo, square_hi)
        high, low = split(fifth)
        pow_hi[side] = high
        pow_lo[side] = low

    @pl.when(jnp.logical_not(diagonal))
    def _():
        pl.semaphore_wait(go_sem, 1)

    @pl.loop(1, N)
    def _(k):
        pltpu.make_async_remote_copy(
            part, parts.at[r], part_send, part_recv, device_id=(e, lax.rem(r + k, N)), device_id_type=MESH
        ).start()

    wait_bytes(block, scat_recv)
    g = block[...].reshape(BLK, BLK)
    half[...] = dot(root[0], g).astype(BF16)
    squares = jnp.zeros((8, BLK), F32)
    for j in range(4):
        step = dot(half[j * 128 : (j + 1) * 128, :], root[1])
        wide[j * 128 : (j + 1) * 128, :] = step
        squares = squares + jnp.sum((step * step).reshape(16, 8, BLK), axis=0)
    norm = jnp.sum(jnp.sum(squares, axis=0, keepdims=True), axis=1, keepdims=True)
    scale = 1.0 / jnp.sqrt(norm + 1e-06)
    for j in range(4):
        step = (wide[j * 128 : (j + 1) * 128, :] * scale).astype(BF16)
        shaped[j * 4 : (j + 1) * 4] = step.reshape(4, ROWS, BLK)

    @pl.loop(0, N)
    def _(k):
        q = lax.rem(lax.rem(r, 4) * 4 + r // 4 + k + e, N)
        i = lax.rem(q, 4) * 4 + q // 4

        @pl.when(i != r)
        def _():
            pltpu.make_async_remote_copy(
                shaped.at[i], passing.at[k], hop_send, hop_recv.at[k], device_id=(e, i), device_id_type=MESH
            ).start()

        @pl.when(i == r)
        def _():
            pltpu.make_async_copy(shaped.at[i], passing.at[k], hop_recv.at[k]).start()

    loads[4].wait()
    stat_new[0] = 0.95 * stat[0] + (0.05 / BLK) * dot(g, g, ((1,), (1,)))

    @pl.loop(0, N)
    def _(k):
        q = lax.rem(lax.rem(r, 4) * 4 + r // 4 + 2 * N - k - e, N)
        f = lax.rem(q, 4) * 4 + q // 4
        wait_bytes(passing.at[k], hop_recv.at[k])

        @pl.when(f != e)
        def _():
            pltpu.make_async_remote_copy(
                passing.at[k], home.at[e], home_send, home_recv, device_id=(f, r), device_id_type=MESH
            ).start()

        @pl.when(f == e)
        def _():
            pltpu.make_async_copy(passing.at[k], home.at[e], home_recv).start()

    loads[5].wait()
    stat_new[1] = 0.95 * stat[1] + (0.05 / BLK) * dot(g, g, ((0,), (0,)))

    @pl.loop(0, 2)
    def _(side):
        stat_hi, stat_lo = split(stat_new[side])
        product = dot(pow_hi[side], stat_hi) + dot(pow_hi[side], stat_lo) + dot(pow_lo[side], stat_hi)
        root_new[side] = (0.25 * (5.0 * root[side].astype(F32) - product)).astype(BF16)

    wait_bytes(parts.at[pl.ds(0, N - 1)], part_recv)
    total = jnp.sum(parts[...], axis=0)
    column = jnp.sum(jnp.where(diag_mask, total, 0.0), axis=1, keepdims=True)
    factor[...] = jnp.broadcast_to(jnp.sqrt(column), (N, BLK))

    wait_bytes(parts.at[pl.ds(0, N - 1)], part_send)

    @pl.when(diagonal)
    def _():
        wait_bytes(staged.at[pl.ds(0, N - 1)], scat_send)

    @pl.when(jnp.logical_not(diagonal))
    def _():
        wait_bytes(staged, scat_send)

    wait_bytes(shaped.at[pl.ds(0, N - 1)], hop_send)
    wait_bytes(passing.at[pl.ds(0, N - 1)], home_send)
    wait_bytes(home, home_recv)


def finish_kernel(
    order_hbm, home, factor, second_new, stat_new, root_new,
    direction, second_out, lstat_out, rstat_out, lroot_out, rroot_out,
    order, wide, sems,
):
    load = pltpu.make_async_copy(order_hbm, order, sems.at[6])
    load.start()
    copies = [
        pltpu.make_async_copy(second_new, second_out, sems.at[0]),
        pltpu.make_async_copy(stat_new.at[0], lstat_out, sems.at[1]),
        pltpu.make_async_copy(stat_new.at[1], rstat_out, sems.at[2]),
        pltpu.make_async_copy(root_new.at[0], lroot_out, sems.at[3]),
        pltpu.make_async_copy(root_new.at[1], rroot_out, sems.at[4]),
    ]
    for copy in copies:
        copy.start()

    load.wait()

    @pl.loop(0, N)
    def _(i):
        j = order[0, i]
        wide[j] = home[i].astype(F32) * factor[pl.ds(j, 1), :]
        pltpu.make_async_copy(wide.at[j], direction.at[j], sems.at[5]).start()

    for copy in copies:
        copy.wait()
    pltpu.make_async_copy(wide, direction, sems.at[5]).wait()


def local(grad_blocks, second_moment, block_order, left_stat, right_stat, left_root, right_root):
    order = pltpu.with_memory_space_constraint(block_order, pltpu.HBM)
    any_spec = pl.BlockSpec(memory_space=pl.ANY)
    hbm_spec = pl.BlockSpec(memory_space=pltpu.HBM)
    vmem_spec = pl.BlockSpec(memory_space=pltpu.VMEM)
    dma = pltpu.SemaphoreType.DMA
    piece = (N, ROWS, BLK)
    pair = (2, BLK, BLK)
    products = 2 * BLK**3
    results = pl.pallas_call(
        exchange_kernel,
        out_shape=[
            pltpu.VMEM(piece, BF16),
            pltpu.VMEM((N, BLK), F32),
            pltpu.VMEM(piece, F32),
            pltpu.VMEM(pair, F32),
            pltpu.VMEM(pair, BF16),
        ],
        in_specs=[hbm_spec] * 7,
        out_specs=[vmem_spec] * 5,
        scratch_shapes=[
            pltpu.SMEM((1, N), jnp.int32),
            pltpu.VMEM(piece, BF16),
            pltpu.VMEM(piece, F32),
            pltpu.VMEM(pair, F32),
            pltpu.VMEM(pair, BF16),
            pltpu.VMEM(piece, BF16),
            pltpu.VMEM(piece, BF16),
            pltpu.VMEM((BLK, BLK), BF16),
            pltpu.VMEM((BLK, BLK), F32),
            pltpu.VMEM(piece, BF16),
            pltpu.VMEM(piece, BF16),
            pltpu.VMEM((N, BLK), F32),
            pltpu.VMEM((1, 128), F32),
            pltpu.VMEM((N, 1, 128), F32),
            pltpu.VMEM(pair, BF16),
            pltpu.VMEM(pair, BF16),
            dma((7,)),
            dma,
            dma,
            dma,
            dma((N,)),
            dma,
            dma,
            dma,
            dma,
            pltpu.SemaphoreType.REGULAR,
            pltpu.SemaphoreType.REGULAR,
        ],
        compiler_params=pltpu.CompilerParams(
            collective_id=0, has_side_effects=True, vmem_limit_bytes=32 * 1024 * 1024
        ),
        cost_estimate=pl.CostEstimate(flops=22 * products, bytes_accessed=10 * 2**20, transcendentals=2**19),
        name="exchange",
    )(
        order,
        *(
            pltpu.with_memory_space_constraint(x[0], pltpu.HBM)
            for x in (grad_blocks, second_moment, left_stat, right_stat, left_root, right_root)
        ),
    )
    outs = pl.pallas_call(
        finish_kernel,
        out_shape=[
            jax.ShapeDtypeStruct(piece, F32),
            jax.ShapeDtypeStruct(piece, F32),
            jax.ShapeDtypeStruct((BLK, BLK), F32),
            jax.ShapeDtypeStruct((BLK, BLK), F32),
            jax.ShapeDtypeStruct((BLK, BLK), BF16),
            jax.ShapeDtypeStruct((BLK, BLK), BF16),
        ],
        in_specs=[hbm_spec] + [vmem_spec] * 5,
        out_specs=[any_spec] * 6,
        scratch_shapes=[pltpu.SMEM((1, N), jnp.int32), pltpu.VMEM(piece, F32), dma((7,))],
        compiler_params=pltpu.CompilerParams(vmem_limit_bytes=32 * 1024 * 1024),
        cost_estimate=pl.CostEstimate(flops=2**19, bytes_accessed=10 * 2**20, transcendentals=0),
        name="finish",
    )(order, *results)
    return tuple(out[None] for out in outs)


def solution(mesh):
    placed = (
        P("expert", None, "fsdp", None),
        P("expert", None, "fsdp", None),
        P("expert", None),
        P(("expert", "fsdp"), None, None),
        P(("expert", "fsdp"), None, None),
        P(("expert", "fsdp"), None, None),
        P(("expert", "fsdp"), None, None),
    )
    return jax.shard_map(
        local,
        mesh=mesh,
        in_specs=placed,
        out_specs=(
            P("expert", None, "fsdp", None),
            P("expert", None, "fsdp", None),
            P(("expert", "fsdp"), None, None),
            P(("expert", "fsdp"), None, None),
            P(("expert", "fsdp"), None, None),
            P(("expert", "fsdp"), None, None),
        ),
        check_vma=False,
    )
```

```python
import functools

import jax
import jax.numpy as jnp
from jax import lax
from jax.experimental import pallas as pl
from jax.experimental.pallas import tpu as pltpu
from jax.sharding import PartitionSpec as P

MESH = pl.DeviceIdType.MESH
N = 16
ROWS = 32
BLK = 512
F32 = jnp.float32
BF16 = jnp.bfloat16


def dot(a, b, dims=((1,), (0,))):
    return lax.dot_general(a, b, (dims, ((), ())), preferred_element_type=F32)


def split(x):
    high = x.astype(BF16)
    return high, (x - high.astype(F32)).astype(BF16)


def pick(index, values):
    result = values[-1]
    for at, value in enumerate(values[:-1]):
        result = jnp.where(index == at, value, result)
    return result


def target(step, expert, turn):
    m = lax.rem(step, 4) + turn
    far = pick(lax.rem(m, 4), (4, 3, 5, 6))
    near = pick(lax.rem(m, 4), (2, 1, 7, 0))
    dz = jnp.where(lax.rem(step, 8) < 4, far, near)
    return lax.rem(expert // 2 + dz, 8) * 2 + step // 8


def wait_bytes(ref, sem):
    pltpu.make_async_copy(ref, ref, sem).wait()


def exchange_kernel(
    order_hbm, grad_hbm, second_hbm, lstat_hbm, rstat_hbm, lroot_hbm, rroot_hbm,
    home, factor, second_new, stat_new, root_new,
    order, grad, second, stat, root, staged, block, half, wide, shaped, passing, rows, part, parts, pow_hi, pow_lo,
    load_sem, scat_send, scat_recv, hop_send, hop_recv, home_send, home_recv, part_send, part_recv, here_sem, go_sem,
):
    e = lax.axis_index("expert")
    r = lax.axis_index("fsdp")
    diagonal = e == r
    turn = e // 2 * 2 + 8 * lax.rem(e, 2)

    loads = [
        pltpu.make_async_copy(grad_hbm, grad, load_sem.at[0]),
        pltpu.make_async_copy(second_hbm, second, load_sem.at[1]),
        pltpu.make_async_copy(lroot_hbm, root.at[0], load_sem.at[2]),
        pltpu.make_async_copy(rroot_hbm, root.at[1], load_sem.at[3]),
        pltpu.make_async_copy(lstat_hbm, stat.at[0], load_sem.at[4]),
        pltpu.make_async_copy(rstat_hbm, stat.at[1], load_sem.at[5]),
    ]
    load_order = pltpu.make_async_copy(order_hbm, order, load_sem.at[6])
    load_order.start()
    loads[0].start()

    barrier = pltpu.get_barrier_semaphore()

    @pl.loop(0, N)
    def _(i):
        @pl.when(jnp.logical_not(diagonal & (i == r)))
        def _():
            pl.semaphore_signal(barrier, inc=1, device_id=(r, i), device_id_type=MESH)

    for load in loads[1:]:
        load.start()

    load_order.wait()
    loads[0].wait()

    @pl.loop(0, N)
    def _(i):
        staged[i] = grad[order[0, i]]

    pl.semaphore_wait(barrier, jnp.where(diagonal, N - 1, N))

    @pl.when(jnp.logical_not(diagonal))
    def _():
        pl.semaphore_signal(here_sem, inc=1, device_id=(e, e), device_id_type=MESH)

    @pl.loop(0, N)
    def _(k):
        i = target(k, e, r)
        stays = diagonal & (i == e)

        @pl.when(jnp.logical_not(stays))
        def _():
            pltpu.make_async_remote_copy(
                staged.at[i], block.at[r], scat_send, scat_recv, device_id=(i, e), device_id_type=MESH
            ).start()

        @pl.when(stays)
        def _():
            pltpu.make_async_copy(staged.at[i], block.at[r], scat_recv).start()

    @pl.when(diagonal)
    def _():
        pl.semaphore_wait(here_sem, N - 1)

        @pl.loop(1, N)
        def _(k):
            pl.semaphore_signal(go_sem, inc=1, device_id=(e, lax.rem(r + k, N)), device_id_type=MESH)

    loads[1].wait()

    @pl.loop(0, N)
    def _(j):
        value = grad[j].astype(F32)
        moment = 0.95 * second[j] + 0.05 * value * value
        second_new[j] = moment
        step = value / (jnp.sqrt(moment) + 1e-08)
        rows[pl.ds(j, 1), :] = jnp.sum(step * step, axis=0, keepdims=True)

    diag_mask = lax.broadcasted_iota(jnp.int32, (N, 128), 0) == lax.broadcasted_iota(jnp.int32, (N, 128), 1)
    sums = jnp.sum(rows[...], axis=1, keepdims=True)
    part[...] = jnp.sum(jnp.where(diag_mask, sums, 0.0), axis=0, keepdims=True)
    parts[r] = part[...]

    loads[2].wait()
    loads[3].wait()

    @pl.loop(0, 2)
    def _(side):
        x = root[side]
        square_hi, square_lo = split(dot(x, x))
        cube_hi, cube_lo = split(dot(x, square_hi) + dot(x, square_lo))
        fifth = dot(cube_hi, square_hi) + dot(cube_hi, square_lo) + dot(cube_lo, square_hi)
        high, low = split(fifth)
        pow_hi[side] = high
        pow_lo[side] = low

    @pl.when(jnp.logical_not(diagonal))
    def _():
        pl.semaphore_wait(go_sem, 1)

    @pl.loop(1, N)
    def _(k):
        pltpu.make_async_remote_copy(
            part, parts.at[r], part_send, part_recv, device_id=(e, lax.rem(r + k, N)), device_id_type=MESH
        ).start()

    wait_bytes(block, scat_recv)
    g = block[...].reshape(BLK, BLK)
    half[...] = dot(root[0], g).astype(BF16)
    squares = jnp.zeros((8, BLK), F32)
    for j in range(4):
        step = dot(half[j * 128 : (j + 1) * 128, :], root[1])
        wide[j * 128 : (j + 1) * 128, :] = step
        squares = squares + jnp.sum((step * step).reshape(16, 8, BLK), axis=0)
    norm = jnp.sum(jnp.sum(squares, axis=0, keepdims=True), axis=1, keepdims=True)
    scale = 1.0 / jnp.sqrt(norm + 1e-06)
    for j in range(4):
        step = (wide[j * 128 : (j + 1) * 128, :] * scale).astype(BF16)
        shaped[j * 4 : (j + 1) * 4] = step.reshape(4, ROWS, BLK)

    @pl.loop(0, N)
    def _(k):
        q = lax.rem(lax.rem(r, 4) * 4 + r // 4 + k + turn, N)
        i = lax.rem(q, 4) * 4 + q // 4

        @pl.when(i != r)
        def _():
            pltpu.make_async_remote_copy(
                shaped.at[i], passing.at[k], hop_send, hop_recv.at[k], device_id=(e, i), device_id_type=MESH
            ).start()

        @pl.when(i == r)
        def _():
            pltpu.make_async_copy(shaped.at[i], passing.at[k], hop_recv.at[k]).start()

    loads[4].wait()
    stat_new[0] = 0.95 * stat[0] + (0.05 / BLK) * dot(g, g, ((1,), (1,)))

    @pl.loop(0, N)
    def _(k):
        q = lax.rem(lax.rem(r, 4) * 4 + r // 4 + 3 * N - k - turn, N)
        f = lax.rem(q, 4) * 4 + q // 4
        wait_bytes(passing.at[k], hop_recv.at[k])

        @pl.when(f != e)
        def _():
            pltpu.make_async_remote_copy(
                passing.at[k], home.at[e], home_send, home_recv, device_id=(f, r), device_id_type=MESH
            ).start()

        @pl.when(f == e)
        def _():
            pltpu.make_async_copy(passing.at[k], home.at[e], home_recv).start()

    loads[5].wait()
    stat_new[1] = 0.95 * stat[1] + (0.05 / BLK) * dot(g, g, ((0,), (0,)))

    @pl.loop(0, 2)
    def _(side):
        stat_hi, stat_lo = split(stat_new[side])
        product = dot(pow_hi[side], stat_hi) + dot(pow_hi[side], stat_lo) + dot(pow_lo[side], stat_hi)
        root_new[side] = (0.25 * (5.0 * root[side].astype(F32) - product)).astype(BF16)

    wait_bytes(parts.at[pl.ds(0, N - 1)], part_recv)
    total = jnp.sum(parts[...], axis=0)
    column = jnp.sum(jnp.where(diag_mask, total, 0.0), axis=1, keepdims=True)
    factor[...] = jnp.broadcast_to(jnp.sqrt(column), (N, BLK))

    wait_bytes(parts.at[pl.ds(0, N - 1)], part_send)

    @pl.when(diagonal)
    def _():
        wait_bytes(staged.at[pl.ds(0, N - 1)], scat_send)

    @pl.when(jnp.logical_not(diagonal))
    def _():
        wait_bytes(staged, scat_send)

    wait_bytes(shaped.at[pl.ds(0, N - 1)], hop_send)
    wait_bytes(passing.at[pl.ds(0, N - 1)], home_send)
    wait_bytes(home, home_recv)


def finish_kernel(
    order_hbm, home, factor, second_new, stat_new, root_new,
    direction, second_out, lstat_out, rstat_out, lroot_out, rroot_out,
    order, wide, sems,
):
    load = pltpu.make_async_copy(order_hbm, order, sems.at[6])
    load.start()
    copies = [
        pltpu.make_async_copy(second_new, second_out, sems.at[0]),
        pltpu.make_async_copy(stat_new.at[0], lstat_out, sems.at[1]),
        pltpu.make_async_copy(stat_new.at[1], rstat_out, sems.at[2]),
        pltpu.make_async_copy(root_new.at[0], lroot_out, sems.at[3]),
        pltpu.make_async_copy(root_new.at[1], rroot_out, sems.at[4]),
    ]
    for copy in copies:
        copy.start()

    load.wait()

    @pl.loop(0, N)
    def _(i):
        j = order[0, i]
        wide[j] = home[i].astype(F32) * factor[pl.ds(j, 1), :]
        pltpu.make_async_copy(wide.at[j], direction.at[j], sems.at[5]).start()

    for copy in copies:
        copy.wait()
    pltpu.make_async_copy(wide, direction, sems.at[5]).wait()


def local(grad_blocks, second_moment, block_order, left_stat, right_stat, left_root, right_root):
    order = pltpu.with_memory_space_constraint(block_order, pltpu.HBM)
    any_spec = pl.BlockSpec(memory_space=pl.ANY)
    hbm_spec = pl.BlockSpec(memory_space=pltpu.HBM)
    vmem_spec = pl.BlockSpec(memory_space=pltpu.VMEM)
    dma = pltpu.SemaphoreType.DMA
    piece = (N, ROWS, BLK)
    pair = (2, BLK, BLK)
    products = 2 * BLK**3
    results = pl.pallas_call(
        exchange_kernel,
        out_shape=[
            pltpu.VMEM(piece, BF16),
            pltpu.VMEM((N, BLK), F32),
            pltpu.VMEM(piece, F32),
            pltpu.VMEM(pair, F32),
            pltpu.VMEM(pair, BF16),
        ],
        in_specs=[hbm_spec] * 7,
        out_specs=[vmem_spec] * 5,
        scratch_shapes=[
            pltpu.SMEM((1, N), jnp.int32),
            pltpu.VMEM(piece, BF16),
            pltpu.VMEM(piece, F32),
            pltpu.VMEM(pair, F32),
            pltpu.VMEM(pair, BF16),
            pltpu.VMEM(piece, BF16),
            pltpu.VMEM(piece, BF16),
            pltpu.VMEM((BLK, BLK), BF16),
            pltpu.VMEM((BLK, BLK), F32),
            pltpu.VMEM(piece, BF16),
            pltpu.VMEM(piece, BF16),
            pltpu.VMEM((N, BLK), F32),
            pltpu.VMEM((1, 128), F32),
            pltpu.VMEM((N, 1, 128), F32),
            pltpu.VMEM(pair, BF16),
            pltpu.VMEM(pair, BF16),
            dma((7,)),
            dma,
            dma,
            dma,
            dma((N,)),
            dma,
            dma,
            dma,
            dma,
            pltpu.SemaphoreType.REGULAR,
            pltpu.SemaphoreType.REGULAR,
        ],
        compiler_params=pltpu.CompilerParams(
            collective_id=0, has_side_effects=True, vmem_limit_bytes=32 * 1024 * 1024
        ),
        cost_estimate=pl.CostEstimate(flops=22 * products, bytes_accessed=10 * 2**20, transcendentals=2**19),
        name="exchange",
    )(
        order,
        *(
            pltpu.with_memory_space_constraint(x[0], pltpu.HBM)
            for x in (grad_blocks, second_moment, left_stat, right_stat, left_root, right_root)
        ),
    )
    outs = pl.pallas_call(
        finish_kernel,
        out_shape=[
            jax.ShapeDtypeStruct(piece, F32),
            jax.ShapeDtypeStruct(piece, F32),
            jax.ShapeDtypeStruct((BLK, BLK), F32),
            jax.ShapeDtypeStruct((BLK, BLK), F32),
            jax.ShapeDtypeStruct((BLK, BLK), BF16),
            jax.ShapeDtypeStruct((BLK, BLK), BF16),
        ],
        in_specs=[hbm_spec] + [vmem_spec] * 5,
        out_specs=[any_spec] * 6,
        scratch_shapes=[pltpu.SMEM((1, N), jnp.int32), pltpu.VMEM(piece, F32), dma((7,))],
        compiler_params=pltpu.CompilerParams(vmem_limit_bytes=32 * 1024 * 1024),
        cost_estimate=pl.CostEstimate(flops=2**19, bytes_accessed=10 * 2**20, transcendentals=0),
        name="finish",
    )(order, *results)
    return tuple(out[None] for out in outs)


def solution(mesh):
    placed = (
        P("expert", None, "fsdp", None),
        P("expert", None, "fsdp", None),
        P("expert", None),
        P(("expert", "fsdp"), None, None),
        P(("expert", "fsdp"), None, None),
        P(("expert", "fsdp"), None, None),
        P(("expert", "fsdp"), None, None),
    )
    return jax.shard_map(
        local,
        mesh=mesh,
        in_specs=placed,
        out_specs=(
            P("expert", None, "fsdp", None),
            P("expert", None, "fsdp", None),
            P(("expert", "fsdp"), None, None),
            P(("expert", "fsdp"), None, None),
            P(("expert", "fsdp"), None, None),
            P(("expert", "fsdp"), None, None),
        ),
        check_vma=False,
    )
```
